32 devices in a mesh: leaf: 32 (over z, y, x, core).
Axes of the slice: x: 2, y: 2, z: 4, core: 2. Of those that a mesh axis runs over, the one named last changes fastest.
Arguments:
- charges: bfloat16 [256, 16, 256], P('leaf'), may hold values from -6 to 6
- points: bfloat16 [256, 3, 256], P('leaf'), may hold values from 0 to 2
- near_list: int32 [256, 16], P('leaf'), may hold values from 0 to 255, as said below
- leaf_basis: bfloat16 [256, 64, 256], P('leaf'), may hold values from -0.375 to 0.375
- transfer: bfloat16 [448, 64, 64], P('leaf'), may hold values from -0.625 to 0.625
- coupling: bfloat16 [480, 64, 512], P('leaf'), may hold values from -0.25 to 0.25
- far_list: int32 [480, 8], P('leaf'), may hold values from 0 to 255, as said below
- top_transfer: bfloat16 [2, 64, 64], replicated, may hold values from -0.625 to 0.625
- top_coupling: bfloat16 [4, 64, 64], replicated, may hold values from -0.5 to 0.5
- top_list: int32 [28, 2], replicated, may hold values from 0 to 15, as said below
Outputs:
- potential: float32 [256, 16, 256], P('leaf')
The draws below stay inside these ranges and needn't reach their ends.
Inputs may be any that keep to these rules, and one draw needn't show every extreme that they name: `near_list`: every entry of the row of leaf g names a leaf within 8 of g; slot 0 is g itself; slot 1 is g + 8, or g - 8 where g + 8 is not a leaf. `far_list`: an entry of the row of node i of block d at level l names a node of level l that belongs to block d - 1, d or d + 1, never node i of block d itself. `top_list`: an entry for node m of a coarse level names a node of the same level whose index differs from m by 1 or 2.
All inputs are finite; a program needn't handle non-finite values.
Results may differ from the reference program's by a relative error of at most 0.012.
Values may be sent and summed in bfloat16 or wider, within the bound.
A program may use at most 64 MiB of HBM per device.

```python
import jax
import jax.numpy as jnp
import numpy as np
from jax import lax

LEAF_PTS = 256
RANK = 64
NRHS = 16
LEVELS_DEV = 3
NNEAR = 16
REACH = 8
NFAR = 8
NFARC = 2
LEAF_DEV = 8
LEAVES = 256
NODES = 480
EDGES = 448
TOP_LEVELS = 3
COARSE = 28
N_LEAF = 32


def draw_near_list(key, part):
    key = jax.random.fold_in(key, 11)
    options = jnp.concatenate([jnp.arange(-REACH, 0), jnp.arange(1, REACH)]).astype(jnp.int32)
    scores = jax.random.randint(key, (LEAVES, 2 * REACH - 1), 0, 1 << 20) * (2 * REACH) + jnp.arange(2 * REACH - 1, dtype=jnp.int32)
    order = jnp.argsort(scores, axis=1)
    picked = options[order[:, :NNEAR - 2]]
    leaf_index = jnp.arange(LEAVES, dtype=jnp.int32)[:, None]
    offsets = jnp.concatenate([jnp.zeros((LEAVES, 1), jnp.int32), jnp.full((LEAVES, 1), REACH, jnp.int32), picked], axis=1)
    target = leaf_index + offsets
    outside = (target < 0) | (target >= LEAVES)
    return jnp.where(outside, leaf_index - offsets, target).astype(jnp.int32)


def draw_far_list(key, part):
    key = jax.random.fold_in(key, 23)
    per_dev = 2 * LEAF_DEV - 1
    widths_table = np.concatenate([np.full(LEAF_DEV >> height, LEAF_DEV >> height) for height in range(LEVELS_DEV + 1)]).astype(np.int32)
    places_table = np.concatenate([np.arange(LEAF_DEV >> height) for height in range(LEVELS_DEV + 1)]).astype(np.int32)
    row_index = jnp.arange(NODES, dtype=jnp.int32)
    slot_index = row_index % per_dev
    device_index = (row_index // per_dev)[:, None]
    node_width = jnp.asarray(widths_table)[slot_index][:, None]
    node_place = jnp.asarray(places_table)[slot_index][:, None]
    raw_draw = jax.random.randint(key, (NODES, NFAR), 0, 3 * node_width - 1)
    chosen = raw_draw + (raw_draw >= node_width + node_place).astype(jnp.int32)
    chosen = jnp.where((device_index == 0) & (chosen < node_width), chosen + 2 * node_width, chosen)
    chosen = jnp.where((device_index == N_LEAF - 1) & (chosen >= 2 * node_width), chosen - 2 * node_width, chosen)
    return ((device_index - 1) * node_width + chosen).astype(jnp.int32)


def draw_top_list(key, part):
    key = jax.random.fold_in(key, 37)
    totals_table = np.concatenate([np.full(N_LEAF >> coarse, N_LEAF >> coarse) for coarse in range(1, TOP_LEVELS + 1)]).astype(np.int32)
    ids_table = np.concatenate([np.arange(N_LEAF >> coarse) for coarse in range(1, TOP_LEVELS + 1)]).astype(np.int32)
    node_totals = jnp.asarray(totals_table)[:, None]
    node_ids = jnp.asarray(ids_table)[:, None]
    scores = jax.random.randint(key, (COARSE, 4), 0, 1 << 20) * 4 + jnp.arange(4, dtype=jnp.int32)
    order = jnp.argsort(scores, axis=1)[:, :NFARC]
    moves_table = jnp.array([-2, -1, 1, 2], jnp.int32)
    moves = moves_table[order]
    target = node_ids + moves
    outside = (target < 0) | (target >= node_totals)
    return jnp.where(outside, node_ids - moves, target).astype(jnp.int32)


def block_scale(key, extent, cuts, low, largest):
    def one(position, shards_of):
        steps = jax.random.uniform(jax.random.fold_in(jax.random.fold_in(key, 6), position), (shards_of,), jnp.float32, low / len(cuts), largest / len(cuts))
        return jnp.repeat(jnp.exp(steps), extent[position] // shards_of).reshape((-1,) + (1,) * (len(extent) - position - 1))

    factor_of = one(*cuts[0])
    for cut in cuts[1:]:
        factor_of = factor_of * one(*cut)
    return factor_of


def bell_draw(key, shape, deviation, most, split=(), kind=jnp.bfloat16):
    values = deviation * jax.random.normal(key, shape, jnp.float32)
    if split:
        values = values * block_scale(key, shape, split, -0.22, 0.18)
    return jnp.clip(values, -most, most).astype(kind)


def setup_inputs(seed: int = 0) -> dict:
    streams_of = jax.random.split(jax.random.key(seed), 11)
    charges = bell_draw(streams_of[0], (LEAVES, NRHS, LEAF_PTS), 1.0, 6.0, ((0, 32),))
    points = jnp.clip(2.0 * jax.random.uniform(streams_of[1], (LEAVES, 3, LEAF_PTS), jnp.float32) ** block_scale(streams_of[1], (LEAVES, 3, LEAF_PTS), ((0, 32),), -0.2, 0.2), 0.0, 2.0).astype(jnp.bfloat16)
    near_list = draw_near_list(jax.random.fold_in(streams_of[10], 71), 0)
    leaf_basis = bell_draw(streams_of[3], (LEAVES, RANK, LEAF_PTS), LEAF_PTS ** -0.5, 0.375, ((0, 32),))
    transfer = bell_draw(streams_of[4], (EDGES, RANK, RANK), (3 * RANK // 2) ** -0.5, 0.625, ((0, 32),))
    coupling = bell_draw(streams_of[5], (NODES, RANK, NFAR * RANK), (NFAR * RANK) ** -0.5, 0.25, ((0, 32),))
    far_list = draw_far_list(jax.random.fold_in(streams_of[10], 71), 0)
    top_transfer = bell_draw(streams_of[7], (2, RANK, RANK), (3 * RANK // 2) ** -0.5, 0.625)
    top_coupling = bell_draw(streams_of[8], (4, RANK, RANK), (NFARC * RANK) ** -0.5, 0.5)
    top_list = draw_top_list(jax.random.fold_in(streams_of[10], 71), 0)
    return dict(charges=charges, points=points, near_list=near_list, leaf_basis=leaf_basis, transfer=transfer, coupling=coupling, far_list=far_list, top_transfer=top_transfer, top_coupling=top_coupling, top_list=top_list)


KERNEL_SCALE = 0.01
SOFTENING = 0.05
PRECISE = lax.Precision.HIGHEST

def kernel_tile(targets, sources):
    delta_x = targets[:, None, 0, :, None] - sources[:, :, 0, None, :]
    delta_y = targets[:, None, 1, :, None] - sources[:, :, 1, None, :]
    delta_z = targets[:, None, 2, :, None] - sources[:, :, 2, None, :]
    squared = delta_x * delta_x + delta_y * delta_y + delta_z * delta_z
    return (KERNEL_SCALE * lax.rsqrt(squared + SOFTENING * SOFTENING)).astype(jnp.bfloat16)

def near_field(charges, points, near_list):
    group_size = min(16, LEAVES)
    coords = points.astype(jnp.float32)

    def one_block(start):
        partner_rows = lax.dynamic_slice_in_dim(near_list, start, group_size, 0)
        targets = lax.dynamic_slice_in_dim(coords, start, group_size, 0)
        sources = coords[partner_rows]
        values = charges[partner_rows].astype(jnp.float32)
        kernel_vals = lax.optimization_barrier(kernel_tile(targets, sources)).astype(jnp.float32)
        return jnp.einsum('gsrb,gsab->gra', values, kernel_vals, precision=PRECISE)
    starts = jnp.arange(0, LEAVES, group_size, dtype=jnp.int32)
    return lax.map(one_block, starts).reshape(LEAVES, NRHS, LEAF_PTS)

def expand(running, tree_left, tree_right):
    left_child = jnp.einsum('mrj,kj->mrk', running, tree_left, precision=PRECISE)
    right_child = jnp.einsum('mrj,kj->mrk', running, tree_right, precision=PRECISE)
    return jnp.stack([left_child, right_child], axis=1).reshape(2 * running.shape[0], running.shape[1], running.shape[2])

def far_field(charges, leaf_basis, transfer, coupling, far_list, top_transfer, top_coupling, top_list):
    per_node = 2 * LEAF_DEV - 1
    per_edge = 2 * LEAF_DEV - 2
    couplers = coupling.reshape(N_LEAF, per_node, RANK, NFAR * RANK)
    partners = far_list.reshape(N_LEAF, per_node, NFAR)
    edges = transfer.reshape(N_LEAF, per_edge, RANK, RANK)
    basis_wide = leaf_basis.astype(jnp.float32)
    levels = [jnp.einsum('lrp,lkp->lrk', charges.astype(jnp.float32), basis_wide, precision=PRECISE).astype(jnp.bfloat16)]
    for height in range(LEVELS_DEV):
        node_count = LEAF_DEV >> height
        start = 2 * LEAF_DEV - 2 * node_count
        matrices = edges[:, start:start + node_count].reshape(N_LEAF * node_count, RANK, RANK).astype(jnp.float32)
        lifted = jnp.einsum('crk,ckj->crj', levels[-1].astype(jnp.float32), matrices, precision=PRECISE)
        levels.append((lifted[0::2] + lifted[1::2]).astype(jnp.bfloat16))
    coupled = []
    for height in range(LEVELS_DEV + 1):
        node_count = LEAF_DEV >> height
        start = 2 * LEAF_DEV - 2 * node_count
        coeffs = levels[height].astype(jnp.float32)

        def one_block(pieces, coeffs=coeffs, node_count=node_count):
            partner_rows, matrices = pieces
            fetched = coeffs[partner_rows]
            weights = matrices.astype(jnp.float32).reshape(node_count, RANK, NFAR, RANK)
            return jnp.einsum('msrq,mksq->mrk', fetched, weights, precision=PRECISE)
        blocks = lax.map(one_block, (partners[:, start:start + node_count], couplers[:, start:start + node_count]))
        coupled.append(blocks.reshape(N_LEAF * node_count, NRHS, RANK))
    tree_left = top_transfer[0].astype(jnp.float32)
    tree_right = top_transfer[1].astype(jnp.float32)
    upward = [levels[LEVELS_DEV]]
    for coarse in range(1, TOP_LEVELS + 1):
        children = upward[-1].astype(jnp.float32)
        parent = jnp.einsum('mrk,kj->mrj', children[0::2], tree_left, precision=PRECISE)
        parent = parent + jnp.einsum('mrk,kj->mrj', children[1::2], tree_right, precision=PRECISE)
        upward.append(parent.astype(jnp.bfloat16))
    couple_wide = top_coupling.astype(jnp.float32)
    crossing = []
    for coarse in range(1, TOP_LEVELS + 1):
        node_count = N_LEAF >> coarse
        start = N_LEAF - 2 * node_count
        partner_rows = top_list[start:start + node_count]
        distance = partner_rows - jnp.arange(node_count, dtype=jnp.int32)[:, None]
        which = jnp.where(distance < 0, distance + 2, distance + 1)
        fetched = upward[coarse].astype(jnp.float32)[partner_rows]
        crossing.append(jnp.einsum('msrk,mskj->mrj', fetched, couple_wide[which], precision=PRECISE))
    running = crossing[TOP_LEVELS - 1]
    for coarse in range(TOP_LEVELS - 1, 0, -1):
        running = crossing[coarse - 1] + expand(running, tree_left, tree_right)
    running = coupled[LEVELS_DEV] + expand(running, tree_left, tree_right)
    for height in range(LEVELS_DEV - 1, -1, -1):
        node_count = LEAF_DEV >> height
        start = 2 * LEAF_DEV - 2 * node_count
        matrices = edges[:, start:start + node_count].reshape(N_LEAF * node_count, RANK, RANK).astype(jnp.float32)
        parent = jnp.repeat(running, 2, axis=0)
        running = coupled[height] + jnp.einsum('crj,ckj->crk', parent, matrices, precision=PRECISE)
    return jnp.einsum('lrk,lkp->lrp', running, basis_wide, precision=PRECISE)

def reference(charges, points, near_list, leaf_basis, transfer, coupling, far_list, top_transfer, top_coupling, top_list):
    near_part = near_field(charges, points, near_list)
    far_part = far_field(charges, leaf_basis, transfer, coupling, far_list, top_transfer, top_coupling, top_list)
    return near_part + far_part
```

```python
import functools

import jax
import jax.numpy as jnp
from jax import lax
from jax.experimental import pallas as pl
from jax.experimental.pallas import tpu as pltpu
from jax.sharding import PartitionSpec as P

KERNEL_SCALE = 0.01
SOFTENING = 0.05
F32 = jnp.float32
BF16 = jnp.bfloat16
NT = (((1,), (1,)), ((), ()))
MESH = pl.DeviceIdType.MESH


def dot(a, b):
    return jnp.dot(a, b, preferred_element_type=F32)


def dot_nt(a, b):
    return lax.dot_general(a, b, NT, preferred_element_type=F32)


def split3(s):
    hi = s.astype(BF16).astype(F32)
    rest = s - hi
    mid = rest.astype(BF16).astype(F32)
    return hi, mid, rest - mid


def source_rows(p):
    s = jnp.sum(p * p, axis=0, keepdims=True)
    ones = jnp.ones((3, p.shape[1]), F32)
    zeros = jnp.zeros((7, p.shape[1]), F32)
    return jnp.concatenate([p, *split3(s), ones, zeros], axis=0)


def target_rows(p):
    s = jnp.sum(p * p, axis=0, keepdims=True) + SOFTENING * SOFTENING
    ones = jnp.ones((3, p.shape[1]), F32)
    zeros = jnp.zeros((7, p.shape[1]), F32)
    return jnp.concatenate([-2.0 * p, ones, *split3(s), zeros], axis=0)


def twice(u):
    return jnp.concatenate([u, u], axis=1)


def body(
    n,
    charges,
    points,
    near_list,
    basis,
    transfer,
    coupling,
    far_list,
    top_transfer,
    top_coupling,
    top_list,
    out,
    src,
    rows,
    target,
    counts,
    nodes,
    roots,
    tops,
    near_send,
    near_recv,
    node_send,
    node_recv,
    root_send,
    root_recv,
):
    me = lax.axis_index("leaf")
    leaves, rhs, pts = charges.shape
    rank = basis.shape[1]
    depth = leaves.bit_length() - 1
    slots = 2 * leaves
    starts = [slots - 2 * (leaves >> h) for h in range(depth + 1)]
    levels_up = n.bit_length() - 3

    barrier = pltpu.get_barrier_semaphore()

    def greet(t, carry):
        other = lax.rem(me + t, n)
        pl.semaphore_signal(barrier, inc=1, device_id=(other,), device_id_type=MESH)
        return carry

    lax.fori_loop(1, n, greet, 0)

    for i in range(leaves):
        p = points[i].astype(F32)
        src[leaves + i, :rhs] = charges[i]
        src[leaves + i, rhs:] = source_rows(p).astype(BF16)
        target[i] = target_rows(p).astype(BF16)

    low = lax.broadcasted_iota(jnp.int32, (rhs, 2 * rank), 1) < rank

    for i in range(leaves):
        b = basis[i]
        nodes[slots + i] = dot_nt(charges[i], jnp.concatenate([b, b], axis=0)).astype(BF16)
    for h in range(depth):
        for q in range(leaves >> (h + 1)):
            c = starts[h] + 2 * q
            pair = jnp.where(low, nodes[slots + c], nodes[slots + c + 1])
            e = transfer[c : c + 2].reshape(2 * rank, rank)
            nodes[slots + starts[h + 1] + q] = twice(dot(pair, e)).astype(BF16)
    root = nodes[2 * slots - 2]
    nodes[2 * slots - 1] = root
    roots[me] = root

    pl.semaphore_wait(barrier, n - 1)

    def near_copy(right):
        return pltpu.make_async_remote_copy(
            src_ref=src.at[pl.ds(leaves, leaves)],
            dst_ref=src.at[pl.ds(0 if right else 2 * leaves, leaves)],
            send_sem=near_send.at[right],
            recv_sem=near_recv.at[right],
            device_id=(jnp.minimum(me + 1, n - 1) if right else jnp.maximum(me - 1, 0),),
            device_id_type=MESH,
        )

    def node_copy(right):
        return pltpu.make_async_remote_copy(
            src_ref=nodes.at[pl.ds(slots, slots)],
            dst_ref=nodes.at[pl.ds(0 if right else 2 * slots, slots)],
            send_sem=node_send.at[right],
            recv_sem=node_recv.at[right],
            device_id=(jnp.minimum(me + 1, n - 1) if right else jnp.maximum(me - 1, 0),),
            device_id_type=MESH,
        )

    @pl.when(me < n - 1)
    def _():
        near_copy(1).start()

    @pl.when(me > 0)
    def _():
        near_copy(0).start()

    def send_root(t, carry):
        pltpu.make_async_remote_copy(
            src_ref=nodes.at[2 * slots - 2],
            dst_ref=roots.at[me],
            send_sem=root_send,
            recv_sem=root_recv,
            device_id=(lax.rem(me + t, n),),
            device_id_type=MESH,
        ).start()
        return carry

    lax.fori_loop(1, n, send_root, 0)

    @pl.when(me < n - 1)
    def _():
        node_copy(1).start()

    @pl.when(me > 0)
    def _():
        node_copy(0).start()

    place = near_list[...] - (me - 1) * leaves
    leaf_id = lax.broadcasted_iota(jnp.int32, place.shape, 0)
    own = (place >= leaves) & (place < 2 * leaves)
    column = jnp.where(
        own, place - leaves, place - leaf_id + jnp.where(place < leaves, leaves, 0)
    )
    lane = lax.broadcasted_iota(jnp.int32, (leaves, 128), 1)
    total = jnp.zeros((leaves, 128), F32)
    for s in range(near_list.shape[1]):
        total = total + jnp.where(column[:, s : s + 1] == lane, 1.0, 0.0)
    counts[...] = total.reshape(leaves, 1, 128)

    def tile(source, goal, weight):
        d2 = dot(rows[source], goal)
        k = lax.rsqrt(d2).astype(BF16)
        w = jnp.broadcast_to(weight, (rhs, pts)).astype(BF16)
        return dot(src[source, :rhs] * w, k)

    def turn(i, carry):
        rows[i] = src[i, rhs:].astype(F32).T.astype(BF16)
        return carry

    lax.fori_loop(leaves, 2 * leaves, turn, 0)

    def own_leaf(i, carry):
        goal = target[i]
        weights = counts[i]
        acc = jnp.zeros((rhs, pts), F32)
        for j in range(leaves):
            acc = acc + tile(leaves + j, goal, weights[:, j : j + 1])
        out[i] = acc
        return carry

    lax.fori_loop(0, leaves, own_leaf, 0)

    @pl.when(me > 0)
    def _():
        near_copy(1).wait_recv()

    @pl.when(me == 0)
    def _():
        src[0:leaves] = src[leaves : 2 * leaves]

    @pl.when(me < n - 1)
    def _():
        near_copy(0).wait_recv()

    @pl.when(me == n - 1)
    def _():
        src[2 * leaves : 3 * leaves] = src[leaves : 2 * leaves]

    lax.fori_loop(0, leaves, turn, 0)
    lax.fori_loop(2 * leaves, 3 * leaves, turn, 0)

    def side_leaf(i, carry):
        goal = target[i]
        weights = counts[i]
        acc = out[i]
        for j in range(leaves + 1):
            source = i + j + leaves * ((i + j) // leaves)
            acc = acc + tile(source, goal, weights[:, leaves + j : leaves + j + 1])
        out[i] = acc
        return carry

    lax.fori_loop(0, leaves, side_leaf, 0)

    everyone = pltpu.make_async_remote_copy(
        src_ref=roots.at[pl.ds(0, n - 1)],
        dst_ref=roots.at[pl.ds(0, n - 1)],
        send_sem=root_send,
        recv_sem=root_recv,
        device_id=(lax.rem(me + 1, n),),
        device_id_type=MESH,
    )
    everyone.wait_recv()
    tt = top_transfer[...].reshape(2 * rank, rank)
    level = roots[...]
    for j in range(1, levels_up + 1):
        count = n >> j
        pairs = level.reshape(count, 2, rhs, 2 * rank)
        mixed = jnp.where(low[None], pairs[:, 0], pairs[:, 1]).reshape(count * rhs, 2 * rank)
        level = twice(dot(mixed, tt)).astype(BF16).reshape(count, rhs, 2 * rank)
        base = n - 2 * count
        tops[base : base + count] = level

    running = None
    for j in range(levels_up, 0, -1):
        count = n >> j
        base = n - 2 * count
        m = lax.shift_right_logical(me, j)
        p0 = top_list[base + m, 0]
        p1 = top_list[base + m, 1]
        k0 = jnp.clip(jnp.where(p0 < m, p0 - m + 2, p0 - m + 1), 0, 3)
        k1 = jnp.clip(jnp.where(p1 < m, p1 - m + 2, p1 - m + 1), 0, 3)
        p0 = jnp.clip(p0, 0, count - 1)
        p1 = jnp.clip(p1, 0, count - 1)
        pair = jnp.where(low, tops[base + p0], tops[base + p1])
        mats = jnp.concatenate([top_coupling[k0], top_coupling[k1]], axis=0)
        cross = dot(pair, mats)
        if running is not None:
            cross = cross + dot_nt(running.astype(BF16), top_transfer[lax.rem(m, 2)])
        running = cross
    running = dot_nt(running.astype(BF16), top_transfer[lax.rem(me, 2)])

    @pl.when(me > 0)
    def _():
        node_copy(1).wait_recv()

    @pl.when(me < n - 1)
    def _():
        node_copy(0).wait_recv()

    def couple(h, q):
        row = starts[h] + q
        width = depth - h

        def fetch(s):
            at = far_list[row, s] - (me - 1) * (leaves >> h)
            block = lax.shift_right_logical(jnp.clip(at, 0, (3 * leaves >> h) - 1), width)
            inner = lax.bitwise_and(at, (leaves >> h) - 1)
            return nodes[block * slots + starts[h] + inner]

        wide = [jnp.where(low, fetch(s), fetch(s + 1)) for s in range(0, far_list.shape[1], 2)]
        return dot_nt(jnp.concatenate(wide, axis=1), coupling[row])

    back = [couple(depth, 0) + running]
    for h in range(depth - 1, -1, -1):
        below = []
        for q in range(leaves >> (h + 1)):
            c = starts[h] + 2 * q
            e = transfer[c : c + 2].reshape(2 * rank, rank)
            pushed = dot_nt(back[q].astype(BF16), e)
            below.append(couple(h, 2 * q) + pushed[:, :rank])
            below.append(couple(h, 2 * q + 1) + pushed[:, rank:])
        back = below
    for i in range(leaves):
        out[i] = KERNEL_SCALE * out[i] + dot(back[i].astype(BF16), basis[i])

    everyone.wait_send()

    @pl.when(me < n - 1)
    def _():
        near_copy(1).wait_send()
        node_copy(1).wait_send()

    @pl.when(me > 0)
    def _():
        near_copy(0).wait_send()
        node_copy(0).wait_send()


def solution(mesh):
    n = mesh.shape["leaf"]
    placed = (
        P("leaf", None, None),
        P("leaf", None, None),
        P("leaf", None),
        P("leaf", None, None),
        P("leaf", None, None),
        P("leaf", None, None),
        P("leaf", None),
        P(),
        P(),
        P(),
    )

    def shards(*args):
        leaves, rhs, pts = args[0].shape
        rank = args[3].shape[1]
        slots = 2 * leaves
        vmem = pl.BlockSpec(memory_space=pltpu.VMEM)
        smem = pl.BlockSpec(memory_space=pltpu.SMEM)
        dma = pltpu.SemaphoreType.DMA
        return pl.pallas_call(
            functools.partial(body, n),
            out_shape=jax.ShapeDtypeStruct((leaves, rhs, pts), F32),
            in_specs=[vmem, vmem, vmem, vmem, vmem, vmem, smem, vmem, vmem, smem],
            out_specs=vmem,
            scratch_shapes=[
                pltpu.VMEM((3 * leaves, 2 * rhs, pts), BF16),
                pltpu.VMEM((3 * leaves, pts, 16), BF16),
                pltpu.VMEM((leaves, 16, pts), BF16),
                pltpu.VMEM((leaves, 1, 128), F32),
                pltpu.VMEM((3 * slots, rhs, 2 * rank), BF16),
                pltpu.VMEM((n, rhs, 2 * rank), BF16),
                pltpu.VMEM((n, rhs, 2 * rank), BF16),
                dma((2,)),
                dma((2,)),
                dma((2,)),
                dma((2,)),
                dma(()),
                dma(()),
            ],
            compiler_params=pltpu.CompilerParams(
                collective_id=0, has_side_effects=True, vmem_limit_bytes=40 * 1024 * 1024
            ),
        )(*args)

    return jax.shard_map(
        shards, mesh=mesh, in_specs=placed, out_specs=P("leaf", None, None), check_vma=False
    )
```

```python
import functools

import jax
import jax.numpy as jnp
from jax import lax
from jax.experimental import pallas as pl
from jax.experimental.pallas import tpu as pltpu
from jax.sharding import PartitionSpec as P

KERNEL_SCALE = 0.01
SOFTENING = 0.05
F32 = jnp.float32
BF16 = jnp.bfloat16
NT = (((1,), (1,)), ((), ()))
MESH = pl.DeviceIdType.MESH


def dot(a, b):
    return jnp.dot(a, b, preferred_element_type=F32)


def dot_nt(a, b):
    return lax.dot_general(a, b, NT, preferred_element_type=F32)


def split3(s):
    hi = s.astype(BF16).astype(F32)
    rest = s - hi
    mid = rest.astype(BF16).astype(F32)
    return hi, mid, rest - mid


def source_rows(p):
    s = jnp.sum(p * p, axis=0, keepdims=True)
    ones = jnp.ones((3, p.shape[1]), F32)
    zeros = jnp.zeros((7, p.shape[1]), F32)
    return jnp.concatenate([p, *split3(s), ones, zeros], axis=0)


def target_rows(p):
    s = jnp.sum(p * p, axis=0, keepdims=True) + SOFTENING * SOFTENING
    ones = jnp.ones((3, p.shape[1]), F32)
    zeros = jnp.zeros((7, p.shape[1]), F32)
    return jnp.concatenate([-2.0 * p, ones, *split3(s), zeros], axis=0)


def twice(u):
    return jnp.concatenate([u, u], axis=1)


def body(
    n,
    charges,
    points_hbm,
    near_list_hbm,
    basis_hbm,
    transfer_hbm,
    coupling_hbm,
    far_list_hbm,
    top_transfer_hbm,
    top_coupling_hbm,
    top_list_hbm,
    out,
    points,
    near_list,
    basis,
    transfer,
    coupling,
    far_list,
    top_transfer,
    top_coupling,
    top_list,
    load_sem,
    src,
    rows,
    target,
    counts,
    nodes,
    roots,
    tops,
    near_send,
    near_recv,
    node_send,
    node_recv,
    root_send,
    root_recv,
):
    me = lax.axis_index("leaf")
    leaves, rhs, pts = charges.shape
    rank = basis.shape[1]
    depth = leaves.bit_length() - 1
    slots = 2 * leaves
    starts = [slots - 2 * (leaves >> h) for h in range(depth + 1)]
    levels_up = n.bit_length() - 3

    barrier = pltpu.get_barrier_semaphore()

    def greet(t, carry):
        other = lax.rem(me + t, n)
        pl.semaphore_signal(barrier, inc=1, device_id=(other,), device_id_type=MESH)
        return carry

    lax.fori_loop(1, n, greet, 0)

    loads = {}
    for at, (name, origin, place) in enumerate(
        (
            ("basis", basis_hbm, basis),
            ("charges", charges, src.at[pl.ds(2 * leaves, leaves), pl.ds(0, rhs)]),
            ("points", points_hbm, points),
            ("transfer", transfer_hbm, transfer),
            ("near_list", near_list_hbm, near_list),
            ("top_transfer", top_transfer_hbm, top_transfer),
            ("top_coupling", top_coupling_hbm, top_coupling),
            ("top_list", top_list_hbm, top_list),
            ("far_list", far_list_hbm, far_list),
            ("coupling", coupling_hbm, coupling),
        )
    ):
        loads[name] = pltpu.make_async_copy(origin, place, load_sem.at[at])
        loads[name].start()

    loads["points"].wait()
    loads["charges"].wait()
    for i in range(leaves):
        p = points[:, i].astype(F32)
        src[2 * leaves + i, rhs:] = source_rows(p).astype(BF16)
        target[i] = target_rows(p).astype(BF16)

    low = lax.broadcasted_iota(jnp.int32, (rhs, 2 * rank), 1) < rank

    loads["basis"].wait()
    loads["transfer"].wait()
    for i in range(leaves):
        b = basis[i]
        nodes[slots + i] = dot_nt(src[2 * leaves + i, :rhs], jnp.concatenate([b, b], axis=0)).astype(BF16)
    for h in range(depth):
        for q in range(leaves >> (h + 1)):
            c = starts[h] + 2 * q
            pair = jnp.where(low, nodes[slots + c], nodes[slots + c + 1])
            e = transfer[c : c + 2].reshape(2 * rank, rank)
            nodes[slots + starts[h + 1] + q] = twice(dot(pair, e)).astype(BF16)
    root = nodes[2 * slots - 2]
    nodes[2 * slots - 1] = root
    roots[me] = root

    pl.semaphore_wait(barrier, n - 1)

    def near_copy(right):
        return pltpu.make_async_remote_copy(
            src_ref=src.at[pl.ds(2 * leaves, leaves)],
            dst_ref=src.at[pl.ds(0 if right else leaves, leaves)],
            send_sem=near_send.at[right],
            recv_sem=near_recv.at[right],
            device_id=(jnp.minimum(me + 1, n - 1) if right else jnp.maximum(me - 1, 0),),
            device_id_type=MESH,
        )

    def node_copy(right):
        return pltpu.make_async_remote_copy(
            src_ref=nodes.at[pl.ds(slots, slots)],
            dst_ref=nodes.at[pl.ds(0 if right else 2 * slots, slots)],
            send_sem=node_send.at[right],
            recv_sem=node_recv.at[right],
            device_id=(jnp.minimum(me + 1, n - 1) if right else jnp.maximum(me - 1, 0),),
            device_id_type=MESH,
        )

    @pl.when(me < n - 1)
    def _():
        near_copy(1).start()

    @pl.when(me > 0)
    def _():
        near_copy(0).start()

    def send_root(t, carry):
        pltpu.make_async_remote_copy(
            src_ref=nodes.at[2 * slots - 2],
            dst_ref=roots.at[me],
            send_sem=root_send,
            recv_sem=root_recv,
            device_id=(lax.rem(me + t, n),),
            device_id_type=MESH,
        ).start()
        return carry

    lax.fori_loop(1, n, send_root, 0)

    @pl.when(me < n - 1)
    def _():
        node_copy(1).start()

    @pl.when(me > 0)
    def _():
        node_copy(0).start()

    loads["near_list"].wait()

    place = near_list[...] - (me - 1) * leaves
    leaf_id = lax.broadcasted_iota(jnp.int32, place.shape, 0)
    own = (place >= leaves) & (place < 2 * leaves)
    column = jnp.where(
        own, place - leaves, place - leaf_id + jnp.where(place < leaves, leaves, 0)
    )
    lane = lax.broadcasted_iota(jnp.int32, (leaves, 128), 1)
    total = jnp.zeros((leaves, 128), F32)
    for s in range(near_list.shape[1]):
        total = total + jnp.where(column[:, s : s + 1] == lane, 1.0, 0.0)
    counts[...] = total.reshape(leaves, 1, 128)

    def tiles(first, count, goal, weights):
        d2 = dot(rows[pl.ds(first, count)].reshape(count * pts, 16), goal)
        k = lax.rsqrt(d2).astype(BF16)
        scaled = [
            src[first + j, :rhs] * jnp.broadcast_to(weights[:, j : j + 1], (rhs, pts)).astype(BF16)
            for j in range(count)
        ]
        return dot(jnp.concatenate(scaled, axis=1), k)

    def turn(i, carry):
        rows[i] = src[i, rhs:].astype(F32).T.astype(BF16)
        return carry

    lax.fori_loop(2 * leaves, 3 * leaves, turn, 0)

    def own_leaf(i, carry):
        out[i] = tiles(2 * leaves, leaves, target[i], counts[i])
        return carry

    lax.fori_loop(0, leaves, own_leaf, 0)

    @pl.when(me > 0)
    def _():
        near_copy(1).wait_recv()

    @pl.when(me == 0)
    def _():
        src[0:leaves] = src[2 * leaves : 3 * leaves]

    @pl.when(me < n - 1)
    def _():
        near_copy(0).wait_recv()

    @pl.when(me == n - 1)
    def _():
        src[leaves : 2 * leaves] = src[2 * leaves : 3 * leaves]

    lax.fori_loop(0, 2 * leaves, turn, 0)

    def side_leaf(i, carry):
        weights = counts[i][:, leaves:]
        out[i] = out[i] + tiles(i, leaves + 1, target[i], weights)
        return carry

    lax.fori_loop(0, leaves, side_leaf, 0)

    everyone = pltpu.make_async_remote_copy(
        src_ref=roots.at[pl.ds(0, n - 1)],
        dst_ref=roots.at[pl.ds(0, n - 1)],
        send_sem=root_send,
        recv_sem=root_recv,
        device_id=(lax.rem(me + 1, n),),
        device_id_type=MESH,
    )
    everyone.wait_recv()
    for name in ("top_transfer", "top_coupling", "top_list", "far_list", "coupling"):
        loads[name].wait()
    tt = top_transfer[...].reshape(2 * rank, rank)
    level = roots[...]
    for j in range(1, levels_up + 1):
        count = n >> j
        pairs = level.reshape(count, 2, rhs, 2 * rank)
        mixed = jnp.where(low[None], pairs[:, 0], pairs[:, 1]).reshape(count * rhs, 2 * rank)
        level = twice(dot(mixed, tt)).astype(BF16).reshape(count, rhs, 2 * rank)
        base = n - 2 * count
        tops[base : base + count] = level

    running = None
    for j in range(levels_up, 0, -1):
        count = n >> j
        base = n - 2 * count
        m = lax.shift_right_logical(me, j)
        p0 = top_list[0, base + m]
        p1 = top_list[1, base + m]
        k0 = jnp.clip(jnp.where(p0 < m, p0 - m + 2, p0 - m + 1), 0, 3)
        k1 = jnp.clip(jnp.where(p1 < m, p1 - m + 2, p1 - m + 1), 0, 3)
        p0 = jnp.clip(p0, 0, count - 1)
        p1 = jnp.clip(p1, 0, count - 1)
        pair = jnp.where(low, tops[base + p0], tops[base + p1])
        mats = jnp.concatenate([top_coupling[k0], top_coupling[k1]], axis=0)
        cross = dot(pair, mats)
        if running is not None:
            cross = cross + dot_nt(running.astype(BF16), top_transfer[lax.rem(m, 2)])
        running = cross
    running = dot_nt(running.astype(BF16), top_transfer[lax.rem(me, 2)])

    @pl.when(me > 0)
    def _():
        node_copy(1).wait_recv()

    @pl.when(me < n - 1)
    def _():
        node_copy(0).wait_recv()

    def couple(h, q):
        row = starts[h] + q
        width = depth - h

        def fetch(s):
            at = far_list[s, row] - (me - 1) * (leaves >> h)
            block = lax.shift_right_logical(jnp.clip(at, 0, (3 * leaves >> h) - 1), width)
            inner = lax.bitwise_and(at, (leaves >> h) - 1)
            return nodes[block * slots + starts[h] + inner]

        wide = [jnp.where(low, fetch(s), fetch(s + 1)) for s in range(0, far_list.shape[0], 2)]
        return dot_nt(jnp.concatenate(wide, axis=1), coupling[row])

    back = [couple(depth, 0) + running]
    for h in range(depth - 1, -1, -1):
        below = []
        for q in range(leaves >> (h + 1)):
            c = starts[h] + 2 * q
            e = transfer[c : c + 2].reshape(2 * rank, rank)
            pushed = dot_nt(back[q].astype(BF16), e)
            below.append(couple(h, 2 * q) + pushed[:, :rank])
            below.append(couple(h, 2 * q + 1) + pushed[:, rank:])
        back = below
    for i in range(leaves):
        out[i] = KERNEL_SCALE * out[i] + dot(back[i].astype(BF16), basis[i])

    everyone.wait_send()

    @pl.when(me < n - 1)
    def _():
        near_copy(1).wait_send()
        node_copy(1).wait_send()

    @pl.when(me > 0)
    def _():
        near_copy(0).wait_send()
        node_copy(0).wait_send()


def solution(mesh):
    n = mesh.shape["leaf"]
    placed = (
        P("leaf", None, None),
        P("leaf", None, None),
        P("leaf", None),
        P("leaf", None, None),
        P("leaf", None, None),
        P("leaf", None, None),
        P("leaf", None),
        P(),
        P(),
        P(),
    )

    def shards(
        charges,
        points,
        near_list,
        basis,
        transfer,
        coupling,
        far_list,
        top_transfer,
        top_coupling,
        top_list,
    ):
        args = (
            charges,
            jnp.transpose(points, (1, 0, 2)),
            near_list,
            basis,
            transfer,
            coupling,
            far_list.T,
            top_transfer,
            top_coupling,
            top_list.T,
        )
        leaves, rhs, pts = charges.shape
        rank = basis.shape[1]
        slots = 2 * leaves
        vmem = pl.BlockSpec(memory_space=pltpu.VMEM)
        hbm = pl.BlockSpec(memory_space=pltpu.HBM)

        def held(kind, array):
            return kind(array.shape, array.dtype)

        dma = pltpu.SemaphoreType.DMA
        return pl.pallas_call(
            functools.partial(body, n),
            out_shape=jax.ShapeDtypeStruct((leaves, rhs, pts), F32),
            in_specs=[hbm] * len(args),
            out_specs=vmem,
            scratch_shapes=[
                *(
                    held(pltpu.SMEM if at in (6, 9) else pltpu.VMEM, args[at])
                    for at in range(1, len(args))
                ),
                dma((len(args),)),
                pltpu.VMEM((3 * leaves, 2 * rhs, pts), BF16),
                pltpu.VMEM((3 * leaves, pts, 16), BF16),
                pltpu.VMEM((leaves, 16, pts), BF16),
                pltpu.VMEM((leaves, 1, 128), F32),
                pltpu.VMEM((3 * slots, rhs, 2 * rank), BF16),
                pltpu.VMEM((n, rhs, 2 * rank), BF16),
                pltpu.VMEM((n, rhs, 2 * rank), BF16),
                dma((2,)),
                dma((2,)),
                dma((2,)),
                dma((2,)),
                dma(()),
                dma(()),
            ],
            compiler_params=pltpu.CompilerParams(
                collective_id=0, has_side_effects=True, vmem_limit_bytes=63 * 1024 * 1024
            ),
        )(*args)

    return jax.shard_map(
        shards, mesh=mesh, in_specs=placed, out_specs=P("leaf", None, None), check_vma=False
    )
```

```python
import functools

import jax
import jax.numpy as jnp
from jax import lax
from jax.experimental import pallas as pl
from jax.experimental.pallas import tpu as pltpu
from jax.sharding import PartitionSpec as P

KERNEL_SCALE = 0.01
SOFTENING = 0.05
F32 = jnp.float32
BF16 = jnp.bfloat16
NT = (((1,), (1,)), ((), ()))
MESH = pl.DeviceIdType.MESH


def dot(a, b):
    return jnp.dot(a, b, preferred_element_type=F32)


def dot_nt(a, b):
    return lax.dot_general(a, b, NT, preferred_element_type=F32)


def split3(s):
    hi = s.astype(BF16).astype(F32)
    rest = s - hi
    mid = rest.astype(BF16).astype(F32)
    return hi, mid, rest - mid


def source_rows(p):
    s = jnp.sum(p * p, axis=0, keepdims=True)
    ones = jnp.ones((3, p.shape[1]), F32)
    zeros = jnp.zeros((7, p.shape[1]), F32)
    return jnp.concatenate([p, *split3(s), ones, zeros], axis=0)


def target_rows(p):
    s = jnp.sum(p * p, axis=0, keepdims=True) + SOFTENING * SOFTENING
    ones = jnp.ones((3, p.shape[1]), F32)
    zeros = jnp.zeros((7, p.shape[1]), F32)
    return jnp.concatenate([-2.0 * p, ones, *split3(s), zeros], axis=0)


def twice(u):
    return jnp.concatenate([u, u], axis=1)


def body(
    n,
    charges,
    points_hbm,
    near_list_hbm,
    basis_hbm,
    transfer_hbm,
    coupling_hbm,
    far_list_hbm,
    top_transfer_hbm,
    top_coupling_hbm,
    top_list_hbm,
    out,
    points,
    near_list,
    basis,
    transfer,
    coupling,
    far_list,
    top_transfer,
    top_coupling,
    top_list,
    load_sem,
    src,
    rows,
    target,
    counts,
    nodes,
    roots,
    tops,
    near_send,
    near_recv,
    node_send,
    node_recv,
    root_send,
    root_recv,
):
    me = lax.axis_index("leaf")
    leaves, rhs, pts = charges.shape
    rank = basis.shape[1]
    depth = leaves.bit_length() - 1
    slots = 2 * leaves
    starts = [slots - 2 * (leaves >> h) for h in range(depth + 1)]
    levels_up = n.bit_length() - 3

    barrier = pltpu.get_barrier_semaphore()

    def greet(t, carry):
        other = lax.rem(me + t, n)
        pl.semaphore_signal(barrier, inc=1, device_id=(other,), device_id_type=MESH)
        return carry

    lax.fori_loop(1, n, greet, 0)

    loads = {}
    for at, (name, origin, place) in enumerate(
        (
            ("basis", basis_hbm, basis),
            ("charges", charges, src.at[pl.ds(2 * leaves, leaves), pl.ds(0, rhs)]),
            ("points", points_hbm, points),
            ("transfer", transfer_hbm, transfer),
            ("near_list", near_list_hbm, near_list),
            ("top_transfer", top_transfer_hbm, top_transfer),
            ("top_coupling", top_coupling_hbm, top_coupling),
            ("top_list", top_list_hbm, top_list),
            ("far_list", far_list_hbm, far_list),
            ("coupling", coupling_hbm, coupling),
        )
    ):
        loads[name] = pltpu.make_async_copy(origin, place, load_sem.at[at])
        loads[name].start()

    loads["points"].wait()
    loads["charges"].wait()
    for i in range(leaves):
        p = points[:, i].astype(F32)
        src[2 * leaves + i, rhs:] = source_rows(p).astype(BF16)
        target[i] = target_rows(p).astype(BF16)

    low = lax.broadcasted_iota(jnp.int32, (rhs, 2 * rank), 1) < rank

    loads["basis"].wait()
    loads["transfer"].wait()
    for i in range(leaves):
        b = basis[i]
        nodes[slots + i] = dot_nt(src[2 * leaves + i, :rhs], jnp.concatenate([b, b], axis=0)).astype(BF16)
    for h in range(depth):
        for q in range(leaves >> (h + 1)):
            c = starts[h] + 2 * q
            pair = jnp.where(low, nodes[slots + c], nodes[slots + c + 1])
            e = transfer[c : c + 2].reshape(2 * rank, rank)
            nodes[slots + starts[h + 1] + q] = twice(dot(pair, e)).astype(BF16)
    root = nodes[2 * slots - 2]
    nodes[2 * slots - 1] = root
    roots[me] = root

    pl.semaphore_wait(barrier, n - 1)

    def near_copy(right):
        return pltpu.make_async_remote_copy(
            src_ref=src.at[pl.ds(2 * leaves, leaves)],
            dst_ref=src.at[pl.ds(0 if right else leaves, leaves)],
            send_sem=near_send.at[right],
            recv_sem=near_recv.at[right],
            device_id=(jnp.minimum(me + 1, n - 1) if right else jnp.maximum(me - 1, 0),),
            device_id_type=MESH,
        )

    def node_copy(right):
        return pltpu.make_async_remote_copy(
            src_ref=nodes.at[pl.ds(slots, slots)],
            dst_ref=nodes.at[pl.ds(0 if right else 2 * slots, slots)],
            send_sem=node_send.at[right],
            recv_sem=node_recv.at[right],
            device_id=(jnp.minimum(me + 1, n - 1) if right else jnp.maximum(me - 1, 0),),
            device_id_type=MESH,
        )

    @pl.when(me < n - 1)
    def _():
        near_copy(1).start()

    @pl.when(me > 0)
    def _():
        near_copy(0).start()

    def send_root(t, carry):
        pltpu.make_async_remote_copy(
            src_ref=nodes.at[2 * slots - 2],
            dst_ref=roots.at[me],
            send_sem=root_send,
            recv_sem=root_recv,
            device_id=(lax.rem(me + t, n),),
            device_id_type=MESH,
        ).start()
        return carry

    lax.fori_loop(1, n, send_root, 0)

    @pl.when(me < n - 1)
    def _():
        node_copy(1).start()

    @pl.when(me > 0)
    def _():
        node_copy(0).start()

    loads["near_list"].wait()

    place = near_list[...] - (me - 1) * leaves
    leaf_id = lax.broadcasted_iota(jnp.int32, place.shape, 0)
    own = (place >= leaves) & (place < 2 * leaves)
    column = jnp.where(
        own, place - leaves, place - leaf_id + jnp.where(place < leaves, leaves, 0)
    )
    lane = lax.broadcasted_iota(jnp.int32, (leaves, 128), 1)
    total = jnp.zeros((leaves, 128), F32)
    for s in range(near_list.shape[1]):
        total = total + jnp.where(column[:, s : s + 1] == lane, 1.0, 0.0)
    counts[...] = total.reshape(leaves, 1, 128)

    def tiles(first, count, goal, weights):
        scaled = [
            src[first + j, :rhs] * jnp.broadcast_to(weights[:, j : j + 1], (rhs, pts)).astype(BF16)
            for j in range(count)
        ]
        total = None
        for j in range(0, count, 3):
            some = min(3, count - j)
            d2 = dot(rows[pl.ds(first + j, some)].reshape(some * pts, 16), goal)
            k = lax.rsqrt(d2).astype(BF16)
            part = dot(jnp.concatenate(scaled[j : j + some], axis=1), k)
            total = part if total is None else total + part
        return total

    def turn(i, carry):
        rows[i] = src[i, rhs:].astype(F32).T.astype(BF16)
        return carry

    lax.fori_loop(2 * leaves, 3 * leaves, turn, 0, unroll=8)

    def own_leaf(i, carry):
        out[i] = tiles(2 * leaves, leaves, target[i], counts[i])
        return carry

    lax.fori_loop(0, leaves, own_leaf, 0, unroll=2)

    @pl.when(me > 0)
    def _():
        near_copy(1).wait_recv()

    @pl.when(me == 0)
    def _():
        src[0:leaves] = src[2 * leaves : 3 * leaves]

    @pl.when(me < n - 1)
    def _():
        near_copy(0).wait_recv()

    @pl.when(me == n - 1)
    def _():
        src[leaves : 2 * leaves] = src[2 * leaves : 3 * leaves]

    lax.fori_loop(0, 2 * leaves, turn, 0, unroll=8)

    def side_leaf(i, carry):
        weights = counts[i][:, leaves:]
        out[i] = out[i] + tiles(i, leaves + 1, target[i], weights)
        return carry

    lax.fori_loop(0, leaves, side_leaf, 0, unroll=2)

    everyone = pltpu.make_async_remote_copy(
        src_ref=roots.at[pl.ds(0, n - 1)],
        dst_ref=roots.at[pl.ds(0, n - 1)],
        send_sem=root_send,
        recv_sem=root_recv,
        device_id=(lax.rem(me + 1, n),),
        device_id_type=MESH,
    )
    everyone.wait_recv()
    for name in ("top_transfer", "top_coupling", "top_list", "far_list", "coupling"):
        loads[name].wait()
    tt = top_transfer[...].reshape(2 * rank, rank)
    level = roots[...]
    for j in range(1, levels_up + 1):
        count = n >> j
        pairs = level.reshape(count, 2, rhs, 2 * rank)
        mixed = jnp.where(low[None], pairs[:, 0], pairs[:, 1]).reshape(count * rhs, 2 * rank)
        level = twice(dot(mixed, tt)).astype(BF16).reshape(count, rhs, 2 * rank)
        base = n - 2 * count
        tops[base : base + count] = level

    running = None
    for j in range(levels_up, 0, -1):
        count = n >> j
        base = n - 2 * count
        m = lax.shift_right_logical(me, j)
        p0 = top_list[0, base + m]
        p1 = top_list[1, base + m]
        k0 = jnp.clip(jnp.where(p0 < m, p0 - m + 2, p0 - m + 1), 0, 3)
        k1 = jnp.clip(jnp.where(p1 < m, p1 - m + 2, p1 - m + 1), 0, 3)
        p0 = jnp.clip(p0, 0, count - 1)
        p1 = jnp.clip(p1, 0, count - 1)
        pair = jnp.where(low, tops[base + p0], tops[base + p1])
        mats = jnp.concatenate([top_coupling[k0], top_coupling[k1]], axis=0)
        cross = dot(pair, mats)
        if running is not None:
            cross = cross + dot_nt(running.astype(BF16), top_transfer[lax.rem(m, 2)])
        running = cross
    running = dot_nt(running.astype(BF16), top_transfer[lax.rem(me, 2)])

    @pl.when(me > 0)
    def _():
        node_copy(1).wait_recv()

    @pl.when(me < n - 1)
    def _():
        node_copy(0).wait_recv()

    def couple(h, q):
        row = starts[h] + q
        width = depth - h

        def fetch(s):
            at = far_list[s, row] - (me - 1) * (leaves >> h)
            block = lax.shift_right_logical(jnp.clip(at, 0, (3 * leaves >> h) - 1), width)
            inner = lax.bitwise_and(at, (leaves >> h) - 1)
            return nodes[block * slots + starts[h] + inner]

        wide = [jnp.where(low, fetch(s), fetch(s + 1)) for s in range(0, far_list.shape[0], 2)]
        return dot_nt(jnp.concatenate(wide, axis=1), coupling[row])

    back = [couple(depth, 0) + running]
    for h in range(depth - 1, -1, -1):
        below = []
        for q in range(leaves >> (h + 1)):
            c = starts[h] + 2 * q
            e = transfer[c : c + 2].reshape(2 * rank, rank)
            pushed = dot_nt(back[q].astype(BF16), e)
            below.append(couple(h, 2 * q) + pushed[:, :rank])
            below.append(couple(h, 2 * q + 1) + pushed[:, rank:])
        back = below
    for i in range(leaves):
        out[i] = KERNEL_SCALE * out[i] + dot(back[i].astype(BF16), basis[i])

    everyone.wait_send()

    @pl.when(me < n - 1)
    def _():
        near_copy(1).wait_send()
        node_copy(1).wait_send()

    @pl.when(me > 0)
    def _():
        near_copy(0).wait_send()
        node_copy(0).wait_send()


def solution(mesh):
    n = mesh.shape["leaf"]
    placed = (
        P("leaf", None, None),
        P("leaf", None, None),
        P("leaf", None),
        P("leaf", None, None),
        P("leaf", None, None),
        P("leaf", None, None),
        P("leaf", None),
        P(),
        P(),
        P(),
    )

    def shards(
        charges,
        points,
        near_list,
        basis,
        transfer,
        coupling,
        far_list,
        top_transfer,
        top_coupling,
        top_list,
    ):
        args = (
            charges,
            jnp.transpose(points, (1, 0, 2)),
            near_list,
            basis,
            transfer,
            coupling,
            far_list.T,
            top_transfer,
            top_coupling,
            top_list.T,
        )
        leaves, rhs, pts = charges.shape
        rank = basis.shape[1]
        slots = 2 * leaves
        vmem = pl.BlockSpec(memory_space=pltpu.VMEM)
        hbm = pl.BlockSpec(memory_space=pltpu.HBM)

        def held(kind, array):
            return kind(array.shape, array.dtype)

        dma = pltpu.SemaphoreType.DMA
        return pl.pallas_call(
            functools.partial(body, n),
            out_shape=jax.ShapeDtypeStruct((leaves, rhs, pts), F32),
            in_specs=[hbm] * len(args),
            out_specs=vmem,
            scratch_shapes=[
                *(
                    held(pltpu.SMEM if at in (6, 9) else pltpu.VMEM, args[at])
                    for at in range(1, len(args))
                ),
                dma((len(args),)),
                pltpu.VMEM((3 * leaves, 2 * rhs, pts), BF16),
                pltpu.VMEM((3 * leaves, pts, 16), BF16),
                pltpu.VMEM((leaves, 16, pts), BF16),
                pltpu.VMEM((leaves, 1, 128), F32),
                pltpu.VMEM((3 * slots, rhs, 2 * rank), BF16),
                pltpu.VMEM((n, rhs, 2 * rank), BF16),
                pltpu.VMEM((n, rhs, 2 * rank), BF16),
                dma((2,)),
                dma((2,)),
                dma((2,)),
                dma((2,)),
                dma(()),
                dma(()),
            ],
            compiler_params=pltpu.CompilerParams(
                collective_id=0, has_side_effects=True, vmem_limit_bytes=63 * 1024 * 1024
            ),
        )(*args)

    return jax.shard_map(
        shards, mesh=mesh, in_specs=placed, out_specs=P("leaf", None, None), check_vma=False
    )
```

```python
import functools

import jax
import jax.numpy as jnp
from jax import lax
from jax.experimental import pallas as pl
from jax.experimental.pallas import tpu as pltpu
from jax.sharding import PartitionSpec as P

KERNEL_SCALE = 0.01
SOFTENING = 0.05
F32 = jnp.float32
BF16 = jnp.bfloat16
NT = (((1,), (1,)), ((), ()))
MESH = pl.DeviceIdType.MESH


def dot(a, b):
    return jnp.dot(a, b, preferred_element_type=F32)


def dot_nt(a, b):
    return lax.dot_general(a, b, NT, preferred_element_type=F32)


def split3(s):
    hi = s.astype(BF16).astype(F32)
    rest = s - hi
    mid = rest.astype(BF16).astype(F32)
    return hi, mid, rest - mid


def source_rows(p):
    s = jnp.sum(p * p, axis=0, keepdims=True)
    ones = jnp.ones((3, p.shape[1]), F32)
    zeros = jnp.zeros((7, p.shape[1]), F32)
    return jnp.concatenate([p, *split3(s), ones, zeros], axis=0)


def target_rows(p):
    s = jnp.sum(p * p, axis=0, keepdims=True) + SOFTENING * SOFTENING
    ones = jnp.ones((3, p.shape[1]), F32)
    zeros = jnp.zeros((7, p.shape[1]), F32)
    return jnp.concatenate([-2.0 * p, ones, *split3(s), zeros], axis=0)


def twice(u):
    return jnp.concatenate([u, u], axis=1)


def body(
    n,
    charges,
    points_hbm,
    near_list_hbm,
    basis_hbm,
    transfer_hbm,
    coupling_hbm,
    far_list_hbm,
    top_transfer_hbm,
    top_coupling_hbm,
    top_list_hbm,
    out,
    points,
    near_list,
    basis,
    transfer,
    coupling,
    far_list,
    top_transfer,
    top_coupling,
    top_list,
    load_sem,
    src,
    rows,
    target,
    counts,
    nodes,
    roots,
    tops,
    near_send,
    near_recv,
    node_send,
    node_recv,
    root_send,
    root_recv,
):
    me = lax.axis_index("leaf")
    leaves, rhs, pts = charges.shape
    rank = basis.shape[1]
    depth = leaves.bit_length() - 1
    slots = 2 * leaves
    starts = [slots - 2 * (leaves >> h) for h in range(depth + 1)]
    levels_up = n.bit_length() - 3

    barrier = pltpu.get_barrier_semaphore()

    def greet(t, carry):
        other = lax.rem(me + t, n)
        pl.semaphore_signal(barrier, inc=1, device_id=(other,), device_id_type=MESH)
        return carry

    lax.fori_loop(1, n, greet, 0)

    loads = {}
    for at, (name, origin, place) in enumerate(
        (
            ("basis", basis_hbm, basis),
            ("charges", charges, src.at[pl.ds(2 * leaves, leaves), pl.ds(0, rhs)]),
            ("points", points_hbm, points),
            ("transfer", transfer_hbm, transfer),
            ("near_list", near_list_hbm, near_list),
            ("top_transfer", top_transfer_hbm, top_transfer),
            ("top_coupling", top_coupling_hbm, top_coupling),
            ("top_list", top_list_hbm, top_list),
            ("far_list", far_list_hbm, far_list),
            ("coupling", coupling_hbm, coupling),
        )
    ):
        loads[name] = pltpu.make_async_copy(origin, place, load_sem.at[at])
        loads[name].start()

    loads["points"].wait()
    loads["charges"].wait()
    for i in range(leaves):
        p = points[:, i].astype(F32)
        src[2 * leaves + i, rhs:] = source_rows(p).astype(BF16)
        target[i] = target_rows(p).astype(BF16)

    low = lax.broadcasted_iota(jnp.int32, (rhs, 2 * rank), 1) < rank

    loads["basis"].wait()
    loads["transfer"].wait()
    for i in range(leaves):
        b = basis[i]
        nodes[slots + i] = dot_nt(src[2 * leaves + i, :rhs], jnp.concatenate([b, b], axis=0)).astype(BF16)
    for h in range(depth):
        for q in range(leaves >> (h + 1)):
            c = starts[h] + 2 * q
            pair = jnp.where(low, nodes[slots + c], nodes[slots + c + 1])
            e = transfer[c : c + 2].reshape(2 * rank, rank)
            nodes[slots + starts[h + 1] + q] = twice(dot(pair, e)).astype(BF16)
    root = nodes[2 * slots - 2]
    nodes[2 * slots - 1] = root
    roots[me] = root

    pl.semaphore_wait(barrier, n - 1)

    def near_copy(right):
        return pltpu.make_async_remote_copy(
            src_ref=src.at[pl.ds(2 * leaves, leaves)],
            dst_ref=src.at[pl.ds(0 if right else leaves, leaves)],
            send_sem=near_send.at[right],
            recv_sem=near_recv.at[right],
            device_id=(jnp.minimum(me + 1, n - 1) if right else jnp.maximum(me - 1, 0),),
            device_id_type=MESH,
        )

    def node_copy(right):
        return pltpu.make_async_remote_copy(
            src_ref=nodes.at[pl.ds(slots, slots)],
            dst_ref=nodes.at[pl.ds(0 if right else 2 * slots, slots)],
            send_sem=node_send.at[right],
            recv_sem=node_recv.at[right],
            device_id=(jnp.minimum(me + 1, n - 1) if right else jnp.maximum(me - 1, 0),),
            device_id_type=MESH,
        )

    @pl.when(me < n - 1)
    def _():
        near_copy(1).start()

    @pl.when(me > 0)
    def _():
        near_copy(0).start()

    def send_root(t, carry):
        pltpu.make_async_remote_copy(
            src_ref=nodes.at[2 * slots - 2],
            dst_ref=roots.at[me],
            send_sem=root_send,
            recv_sem=root_recv,
            device_id=(lax.rem(me + t, n),),
            device_id_type=MESH,
        ).start()
        return carry

    lax.fori_loop(1, n, send_root, 0)

    @pl.when(me < n - 1)
    def _():
        node_copy(1).start()

    @pl.when(me > 0)
    def _():
        node_copy(0).start()

    loads["near_list"].wait()

    place = near_list[...] - (me - 1) * leaves
    leaf_id = lax.broadcasted_iota(jnp.int32, place.shape, 0)
    own = (place >= leaves) & (place < 2 * leaves)
    column = jnp.where(
        own, place - leaves, place - leaf_id + jnp.where(place < leaves, leaves, 0)
    )
    lane = lax.broadcasted_iota(jnp.int32, (leaves, 128), 1)
    total = jnp.zeros((leaves, 128), F32)
    for s in range(near_list.shape[1]):
        total = total + jnp.where(column[:, s : s + 1] == lane, 1.0, 0.0)
    counts[...] = total.reshape(leaves, 1, 128)

    def tiles(first, count, goal, weights):
        scaled = [
            src[first + j, :rhs] * jnp.broadcast_to(weights[:, j : j + 1], (rhs, pts)).astype(BF16)
            for j in range(count)
        ]
        total = None
        for j in range(0, count, 3):
            some = min(3, count - j)
            d2 = dot(rows[pl.ds(first + j, some)].reshape(some * pts, 16), goal)
            k = lax.rsqrt(d2).astype(BF16)
            part = dot(jnp.concatenate(scaled[j : j + some], axis=1), k)
            total = part if total is None else total + part
        return total

    def turn(i, carry):
        rows[i] = src[i, rhs:].astype(F32).T.astype(BF16)
        return carry

    lax.fori_loop(2 * leaves, 3 * leaves, turn, 0, unroll=8)

    def own_leaf(i, carry):
        out[i] = tiles(2 * leaves, leaves, target[i], counts[i])
        return carry

    lax.fori_loop(0, leaves, own_leaf, 0, unroll=4)

    @pl.when(me > 0)
    def _():
        near_copy(1).wait_recv()

    @pl.when(me == 0)
    def _():
        src[0:leaves] = src[2 * leaves : 3 * leaves]

    @pl.when(me < n - 1)
    def _():
        near_copy(0).wait_recv()

    @pl.when(me == n - 1)
    def _():
        src[leaves : 2 * leaves] = src[2 * leaves : 3 * leaves]

    lax.fori_loop(0, 2 * leaves, turn, 0, unroll=8)

    def side_leaf(i, carry):
        weights = counts[i][:, leaves:]
        out[i] = out[i] + tiles(i, leaves + 1, target[i], weights)
        return carry

    lax.fori_loop(0, leaves, side_leaf, 0, unroll=4)

    everyone = pltpu.make_async_remote_copy(
        src_ref=roots.at[pl.ds(0, n - 1)],
        dst_ref=roots.at[pl.ds(0, n - 1)],
        send_sem=root_send,
        recv_sem=root_recv,
        device_id=(lax.rem(me + 1, n),),
        device_id_type=MESH,
    )
    everyone.wait_recv()
    for name in ("top_transfer", "top_coupling", "top_list", "far_list", "coupling"):
        loads[name].wait()
    tt = top_transfer[...].reshape(2 * rank, rank)
    level = roots[...]
    for j in range(1, levels_up + 1):
        count = n >> j
        pairs = level.reshape(count, 2, rhs, 2 * rank)
        mixed = jnp.where(low[None], pairs[:, 0], pairs[:, 1]).reshape(count * rhs, 2 * rank)
        level = twice(dot(mixed, tt)).astype(BF16).reshape(count, rhs, 2 * rank)
        base = n - 2 * count
        tops[base : base + count] = level

    running = None
    for j in range(levels_up, 0, -1):
        count = n >> j
        base = n - 2 * count
        m = lax.shift_right_logical(me, j)
        p0 = top_list[0, base + m]
        p1 = top_list[1, base + m]
        k0 = jnp.clip(jnp.where(p0 < m, p0 - m + 2, p0 - m + 1), 0, 3)
        k1 = jnp.clip(jnp.where(p1 < m, p1 - m + 2, p1 - m + 1), 0, 3)
        p0 = jnp.clip(p0, 0, count - 1)
        p1 = jnp.clip(p1, 0, count - 1)
        pair = jnp.where(low, tops[base + p0], tops[base + p1])
        mats = jnp.concatenate([top_coupling[k0], top_coupling[k1]], axis=0)
        cross = dot(pair, mats)
        if running is not None:
            cross = cross + dot_nt(running.astype(BF16), top_transfer[lax.rem(m, 2)])
        running = cross
    running = dot_nt(running.astype(BF16), top_transfer[lax.rem(me, 2)])

    @pl.when(me > 0)
    def _():
        node_copy(1).wait_recv()

    @pl.when(me < n - 1)
    def _():
        node_copy(0).wait_recv()

    def couple(h, q):
        row = starts[h] + q
        width = depth - h

        def fetch(s):
            at = far_list[s, row] - (me - 1) * (leaves >> h)
            block = lax.shift_right_logical(jnp.clip(at, 0, (3 * leaves >> h) - 1), width)
            inner = lax.bitwise_and(at, (leaves >> h) - 1)
            return nodes[block * slots + starts[h] + inner]

        wide = [jnp.where(low, fetch(s), fetch(s + 1)) for s in range(0, far_list.shape[0], 2)]
        return dot_nt(jnp.concatenate(wide, axis=1), coupling[row])

    back = [couple(depth, 0) + running]
    for h in range(depth - 1, -1, -1):
        below = []
        for q in range(leaves >> (h + 1)):
            c = starts[h] + 2 * q
            e = transfer[c : c + 2].reshape(2 * rank, rank)
            pushed = dot_nt(back[q].astype(BF16), e)
            below.append(couple(h, 2 * q) + pushed[:, :rank])
            below.append(couple(h, 2 * q + 1) + pushed[:, rank:])
        back = below
    for i in range(leaves):
        out[i] = KERNEL_SCALE * out[i] + dot(back[i].astype(BF16), basis[i])

    everyone.wait_send()

    @pl.when(me < n - 1)
    def _():
        near_copy(1).wait_send()
        node_copy(1).wait_send()

    @pl.when(me > 0)
    def _():
        near_copy(0).wait_send()
        node_copy(0).wait_send()


def solution(mesh):
    n = mesh.shape["leaf"]
    placed = (
        P("leaf", None, None),
        P("leaf", None, None),
        P("leaf", None),
        P("leaf", None, None),
        P("leaf", None, None),
        P("leaf", None, None),
        P("leaf", None),
        P(),
        P(),
        P(),
    )

    def shards(
        charges,
        points,
        near_list,
        basis,
        transfer,
        coupling,
        far_list,
        top_transfer,
        top_coupling,
        top_list,
    ):
        args = (
            charges,
            jnp.transpose(points, (1, 0, 2)),
            near_list,
            basis,
            transfer,
            coupling,
            far_list.T,
            top_transfer,
            top_coupling,
            top_list.T,
        )
        leaves, rhs, pts = charges.shape
        rank = basis.shape[1]
        slots = 2 * leaves
        vmem = pl.BlockSpec(memory_space=pltpu.VMEM)
        hbm = pl.BlockSpec(memory_space=pltpu.HBM)

        def held(kind, array):
            return kind(array.shape, array.dtype)

        dma = pltpu.SemaphoreType.DMA
        return pl.pallas_call(
            functools.partial(body, n),
            out_shape=jax.ShapeDtypeStruct((leaves, rhs, pts), F32),
            in_specs=[hbm] * len(args),
            out_specs=vmem,
            scratch_shapes=[
                *(
                    held(pltpu.SMEM if at in (6, 9) else pltpu.VMEM, args[at])
                    for at in range(1, len(args))
                ),
                dma((len(args),)),
                pltpu.VMEM((3 * leaves, 2 * rhs, pts), BF16),
                pltpu.VMEM((3 * leaves, pts, 16), BF16),
                pltpu.VMEM((leaves, 16, pts), BF16),
                pltpu.VMEM((leaves, 1, 128), F32),
                pltpu.VMEM((3 * slots, rhs, 2 * rank), BF16),
                pltpu.VMEM((n, rhs, 2 * rank), BF16),
                pltpu.VMEM((n, rhs, 2 * rank), BF16),
                dma((2,)),
                dma((2,)),
                dma((2,)),
                dma((2,)),
                dma(()),
                dma(()),
            ],
            compiler_params=pltpu.CompilerParams(
                collective_id=0, has_side_effects=True, vmem_limit_bytes=63 * 1024 * 1024
            ),
        )(*args)

    return jax.shard_map(
        shards, mesh=mesh, in_specs=placed, out_specs=P("leaf", None, None), check_vma=False
    )
```
